32 devices in a mesh: groups: 2 (over y), tile: 4 (over z), row: 2 (over x), lev: 2 (over core).
Axes of the slice: x: 2, y: 2, z: 4, core: 2. Of those that a mesh axis runs over, the one named last changes fastest.
Arguments:
- air_exchange_rates: float32 [8, 1024, 128], P('lev', ('groups', 'tile', 'row')), parts along dimension 1, may hold values from -48 to 48
- outgoing_stripes: int32 [16, 8, 4], P(('groups', 'tile', 'row')), parts along dimension 0, may hold values from 0 to 63
- outgoing_tally: int32 [16, 8], P(('groups', 'tile', 'row')), parts along dimension 0, may hold values from 1 to 4, as said below
- regrid_inputs: int32 [2048, 2, 4], P(('groups', 'tile'), 'row'), parts along dimension 0, may hold values from 0 to 31, as said below
- regrid_factor_id: int32 [2048, 2, 4], P(('groups', 'tile'), 'row'), parts along dimension 0, may hold values from 0 to 15
- regrid_tally: int32 [2048, 2], P(('groups', 'tile'), 'row'), parts along dimension 0, may hold values from 1 to 4, as said below
- intersection_areas: float32 [32, 128, 128], P('groups'), parts along dimension 0, may hold values from 0.002 to 0.014
- sea_indicator: int32 [2048, 256], P(('groups', 'tile'), 'row'), parts along dimension 0, may hold values 0 or 1
- mixing_rate: float32 [2048, 256], P(('groups', 'tile'), 'row'), parts along dimension 0, may hold values from 0.03 to 0.24
- warmth_profile: float32 [16, 2048, 256], P('lev', ('groups', 'tile'), 'row'), parts along dimension 1, may hold values from 0 to 4
- warming_factor: float32 [8, 16], P(None, 'lev'), may hold values from -6 to 6
- stratum_depths: float32 [16], replicated, may hold values from 1 to 10
Outputs:
- warmth_following: float32 [16, 2048, 256], P('lev', ('groups', 'tile'), 'row'), parts along dimension 1
- air_side_skin_heat: float32 [1024, 128], P(('groups', 'tile', 'row')), parts along dimension 0
The draws below stay inside these ranges and needn't reach their ends.
There are 2 independent parts, one for each index of `groups`. The reference program is written for one: setup_inputs(seed, part) draws one part's arguments, and reference() takes and returns one part's arrays. A program takes and returns all parts, laid end to end along the dimension named above; an argument that names none is the same for every part. Nothing has to cross between parts.
Inputs may be any that keep to these rules, and one draw needn't show every extreme that they name: `outgoing_tally`: some ocean tile receives 4 live slots from every owner. `regrid_inputs`: the first listed block (k = 0) of every grid line names a live slot. `regrid_tally`: the first grid line of each tile lists 4 blocks.
All inputs are finite; a program needn't handle non-finite values. No bound on the sum of `sea_indicator` on one device may be relied on, other than what follows from the above.
Results may differ from the reference program's by a relative error of at most 0.0003.
Values sent between devices are 32-bit elements; how exact they have to be, the bound alone decides.
A program may use at most 64 MiB of HBM per device.

```python
import math
import jax
import jax.numpy as jnp
from jax import lax

F = 8
PATCH_EXTENT = 128
NW = 16
KMAX = 4
SLOTS = 4
AROWS = 64
PANEL_STRIPES = 256
PEERS = 8
COLB = 2
MARINE_SPAN_EAST = 1024
MARINE_SPAN_NORTH = 256
DEPTH_STRATA = 16
ATOT = 512


def shared_counts(key):
    level_key, heavy_key, spread_key = jax.random.split(key, 3)
    levels = jax.random.randint(level_key, (PEERS,), 1, SLOTS + 1)
    busiest = jax.random.randint(heavy_key, (), 0, PEERS)
    receiver = jnp.arange(PEERS)
    levels = jnp.where(receiver == busiest, SLOTS, levels)
    spread = jax.random.randint(spread_key, (PEERS, PEERS), 0, 1 << 20)
    counts = 1 + spread % levels[None, :]
    return jnp.where(receiver[None, :] == busiest, SLOTS, counts).astype(jnp.int32)


def draw_outgoing_tally(key, part):
    return shared_counts(key)


def draw_regrid_inputs(key, part):
    counts = shared_counts(key)
    key = jax.random.fold_in(key, 7)
    sender_key, slot_key, live_key = jax.random.split(key, 3)
    grid_shape = (MARINE_SPAN_EAST, COLB, KMAX)
    sender = jax.random.randint(sender_key, grid_shape, 0, PEERS)
    receiver = (jnp.arange(MARINE_SPAN_EAST) // PANEL_STRIPES)[:, None, None] * COLB + jnp.arange(COLB)[None, :, None]
    receiver = jnp.broadcast_to(receiver, grid_shape)
    live_count = counts[sender, receiver]
    any_slot = jax.random.randint(slot_key, grid_shape, 0, SLOTS)
    live_slot = jax.random.randint(live_key, grid_shape, 0, live_count)
    first_block = jnp.arange(KMAX)[None, None, :] == 0
    return (sender * SLOTS + jnp.where(first_block, live_slot, any_slot)).astype(jnp.int32)


def draw_regrid_tally(key, part):
    key = jax.random.fold_in(key, 5)
    level_key, spread_key = jax.random.split(key)
    levels = jax.random.randint(level_key, (MARINE_SPAN_EAST // PANEL_STRIPES, COLB), 1, KMAX + 1)
    spread = jax.random.randint(spread_key, (MARINE_SPAN_EAST, COLB), 0, 1 << 20)
    level_rows = jnp.repeat(levels, PANEL_STRIPES, axis=0)
    counts = 1 + spread % level_rows
    first_line = (jnp.arange(MARINE_SPAN_EAST) % PANEL_STRIPES == 0)[:, None]
    return jnp.where(first_line, KMAX, counts).astype(jnp.int32)


def plant(array, rng, low, high):
    longest = array.shape.index(max(array.shape))
    spots = []
    for shift in (0, 1):
        where = [jax.random.randint(jax.random.fold_in(rng, axis), (), 0, length) for axis, length in enumerate(array.shape)]
        where[longest] = (where[longest] + shift) % array.shape[longest]
        spots.append(tuple(where))
    return array.at[spots[0]].set(low).at[spots[1]].set(high)


def shard_levels(own_key, dims, cuts, least, high):
    level, own = 1.0, jax.random.fold_in(own_key, 6)
    for dim, blocks in cuts:
        heights = jnp.exp(jax.random.uniform(jax.random.fold_in(own, dim), (blocks,), jnp.float32, least / len(cuts), high / len(cuts)))
        level = level * jnp.repeat(heights, dims[dim] // blocks).reshape([-1 if axis == dim else 1 for axis in range(len(dims))])
    return level


def bell_draw(stream_key, shape, scale, bound, shards=(), kind=jnp.bfloat16):
    drawn = scale * jax.random.normal(stream_key, shape, jnp.float32)
    if shards:
        drawn = drawn * shard_levels(stream_key, shape, shards, -0.22, 0.18)
    return jnp.clip(drawn, -bound, bound).astype(kind)


def setup_inputs(seed: int = 0, part: int = 0) -> dict:
    splits = jax.random.split(jax.random.key(seed), 13)
    part_splits = jax.random.split(jax.random.fold_in(splits[12], part), 13)
    return {
        "air_exchange_rates": bell_draw(part_splits[0], (F, ATOT, PATCH_EXTENT), 8.0, 48.0, ((0, 2), (1, 8)), jnp.float32),
        "outgoing_stripes": plant(jax.random.randint(part_splits[1], (PEERS, PEERS, SLOTS), 0, AROWS), jax.random.fold_in(part_splits[1], 1), 0, AROWS - 1).astype(jnp.int32),
        "outgoing_tally": draw_outgoing_tally(jax.random.fold_in(jax.random.fold_in(splits[12], part), 71), part),
        "regrid_inputs": draw_regrid_inputs(jax.random.fold_in(jax.random.fold_in(splits[12], part), 71), part),
        "regrid_factor_id": plant(jax.random.randint(part_splits[4], (MARINE_SPAN_EAST, COLB, KMAX), 0, NW), jax.random.fold_in(part_splits[4], 1), 0, NW - 1).astype(jnp.int32),
        "regrid_tally": draw_regrid_tally(jax.random.fold_in(jax.random.fold_in(splits[12], part), 71), part),
        "intersection_areas": jnp.clip(jax.random.uniform(part_splits[6], (NW, PATCH_EXTENT, PATCH_EXTENT), jnp.float32, 0.002, 0.014), 0.002, 0.014),
        "sea_indicator": plant((jax.random.randint(part_splits[7], (MARINE_SPAN_EAST, MARINE_SPAN_NORTH), 0, 4) < 3).astype(jnp.int32), jax.random.fold_in(part_splits[7], 1), 0, 1),
        "mixing_rate": jnp.clip(jnp.exp(math.log(0.24) - 2.0794415 * jax.random.uniform(part_splits[8], (MARINE_SPAN_EAST, MARINE_SPAN_NORTH), jnp.float32) ** shard_levels(part_splits[8], (MARINE_SPAN_EAST, MARINE_SPAN_NORTH), ((0, 4), (1, 2)), -0.2, 0.2)), 0.03, 0.24),
        "warmth_profile": jnp.clip(4.0 * jax.random.uniform(part_splits[9], (DEPTH_STRATA, MARINE_SPAN_EAST, MARINE_SPAN_NORTH), jnp.float32) ** shard_levels(part_splits[9], (DEPTH_STRATA, MARINE_SPAN_EAST, MARINE_SPAN_NORTH), ((0, 2), (1, 4), (2, 2)), -0.2, 0.2), 0.0, 4.0),
        "warming_factor": bell_draw(splits[10], (F, DEPTH_STRATA), 1.5, 6.0, ((1, 2),), jnp.float32),
        "stratum_depths": jnp.clip(jnp.exp(jax.random.uniform(splits[11], (DEPTH_STRATA,), jnp.float32, math.log(1.0), math.log(10.0))), 1.0, 10.0),
    }


precise = lax.Precision.HIGHEST


def owner_lists(regrid_inputs, regrid_factor_id, regrid_tally, receiver):
    tile_at = (receiver // COLB).astype(jnp.int32)
    col_at = (receiver % COLB).astype(jnp.int32)
    offset_east = (tile_at * PANEL_STRIPES).astype(jnp.int32)
    zero_at = jnp.zeros((), jnp.int32)
    source_slot = lax.dynamic_slice(regrid_inputs, (offset_east, col_at, zero_at), (PANEL_STRIPES, 1, KMAX))[:, 0]
    weight_id = lax.dynamic_slice(regrid_factor_id, (offset_east, col_at, zero_at), (PANEL_STRIPES, 1, KMAX))[:, 0]
    block_count = lax.dynamic_slice(regrid_tally, (offset_east, col_at), (PANEL_STRIPES, 1))[:, 0]
    usable = (jnp.arange(KMAX, dtype=jnp.int32)[None, :] < block_count[:, None]).astype(jnp.float32)
    return source_slot, weight_id, usable, offset_east, (col_at * PATCH_EXTENT).astype(jnp.int32)


def reference(air_exchange_rates, outgoing_stripes, outgoing_tally, regrid_inputs, regrid_factor_id, regrid_tally, intersection_areas, sea_indicator, mixing_rate, warmth_profile, warming_factor, stratum_depths):
    live_mask = (jnp.arange(SLOTS, dtype=jnp.int32)[None, None, :] < outgoing_tally[:, :, None]).astype(jnp.float32)
    atm_blocks = air_exchange_rates.reshape(F, PEERS, AROWS, PATCH_EXTENT)
    sender = jnp.arange(PEERS, dtype=jnp.int32)
    marine_indicator = sea_indicator.astype(jnp.float32)

    def forward_one(receiver):
        row_ids = outgoing_stripes[:, receiver, :]
        gathered = atm_blocks[:, sender[:, None], row_ids, :] * live_mask[:, receiver, :][None, :, :, None]
        slots_flat = gathered.reshape(F, PEERS * SLOTS, PATCH_EXTENT)
        source_slot, weight_id, usable, offset_east, offset_north = owner_lists(regrid_inputs, regrid_factor_id, regrid_tally, receiver)
        chosen = intersection_areas[weight_id]
        fetched = slots_flat[:, source_slot] * usable[None, :, :, None]
        dividend_sum = jnp.einsum("xkec,fxkc->fxe", chosen, fetched, precision=precise)
        coverage = jnp.einsum("xke,xk->xe", jnp.sum(chosen, axis=3), usable, precision=precise)
        return dividend_sum / coverage[None]

    per_owner = lax.map(forward_one, sender)
    tiles = PEERS // COLB
    remapped = per_owner.reshape(tiles, COLB, F, PANEL_STRIPES, PATCH_EXTENT).transpose(2, 0, 3, 1, 4).reshape(F, MARINE_SPAN_EAST, MARINE_SPAN_NORTH)
    thermal_tendency = jnp.einsum("fl,fxy->lxy", warming_factor, remapped, precision=precise)
    piled_arrays = jnp.concatenate([warmth_profile, marine_indicator[None], mixing_rate[None]], axis=0)
    padded = jnp.pad(piled_arrays, ((0, 0), (1, 1), (1, 1)))
    spread_tracer = jnp.zeros_like(warmth_profile)
    for step_x, step_y in ((1, 0), (-1, 0), (0, 1), (0, -1)):
        neighbour_values = padded[:, 1 + step_x:1 + step_x + MARINE_SPAN_EAST, 1 + step_y:1 + step_y + MARINE_SPAN_NORTH]
        spread_tracer = spread_tracer + neighbour_values[DEPTH_STRATA] * 0.5 * (mixing_rate + neighbour_values[DEPTH_STRATA + 1]) * (neighbour_values[:DEPTH_STRATA] - warmth_profile)
    warmth_following = warmth_profile + marine_indicator * (spread_tracer + thermal_tendency)
    topmost_stratum = jnp.einsum("l,lxy->xy", stratum_depths, warmth_following, precision=precise) / jnp.sum(stratum_depths)

    def back_one(totals, receiver):
        source_slot, weight_id, usable, offset_east, offset_north = owner_lists(regrid_inputs, regrid_factor_id, regrid_tally, receiver)
        patch_skin_heat = lax.dynamic_slice(topmost_stratum, (offset_east, offset_north), (PANEL_STRIPES, PATCH_EXTENT))
        patch_sea_indicator = lax.dynamic_slice(marine_indicator, (offset_east, offset_north), (PANEL_STRIPES, PATCH_EXTENT))
        coupled_entries = jnp.stack([patch_sea_indicator * patch_skin_heat, patch_sea_indicator], axis=1)
        chosen = intersection_areas[weight_id]
        contribution = jnp.einsum("xkec,xje->xkjc", chosen, coupled_entries, precision=precise) * usable[:, :, None, None]
        flat_slot = source_slot.reshape(-1)
        from_owner = flat_slot // SLOTS
        slot_at = flat_slot % SLOTS
        row_ids = outgoing_stripes[from_owner, receiver, slot_at]
        weight_live = live_mask[from_owner, receiver, slot_at]
        totals = totals.at[from_owner, row_ids].add(contribution.reshape(PANEL_STRIPES * KMAX, 2, PATCH_EXTENT) * weight_live[:, None, None])
        return totals, None

    totals, unused = lax.scan(back_one, jnp.zeros((PEERS, AROWS, 2, PATCH_EXTENT), jnp.float32), sender)
    joined_parts = totals.reshape(ATOT, 2, PATCH_EXTENT)
    air_side_skin_heat = joined_parts[:, 0] / jnp.maximum(joined_parts[:, 1], 1.0)
    return warmth_following, air_side_skin_heat
```

```python
import functools
import jax
import jax.numpy as jnp
from jax import lax
from jax.experimental import pallas as pl
from jax.experimental.pallas import tpu as pltpu
from jax.sharding import PartitionSpec as P

precise = lax.Precision.HIGHEST
f32 = jnp.float32
bf16 = jnp.bfloat16
MESH = pl.DeviceIdType.MESH
SMALL = 16


def halves(v):
    hi = v.astype(bf16)
    return hi, (v - hi.astype(f32)).astype(bf16)


def iota(shape, dim):
    return lax.broadcasted_iota(jnp.int32, shape, dim)


def dot(a, b):
    return jnp.dot(a, b, preferred_element_type=f32)


def window(
    tiles, rows, levs,
    air_ref, stripes_ref, tally_ref, src_ref, wid_ref, cnt_ref, area_ref, sea_ref, mix_ref,
    warm_ref, factor_ref, thick_ref,
    out_ref, skin_ref,
    outbox, inbox, edge, zin, colbuf, xin, dbuf, sel, sel_t, area_t, area_cat, table, base,
    spread, reply, replies,
    flux_send, flux_recv, halo_send, halo_recv, back_send, back_recv,
):
    tile, row, lev = lax.axis_index("tile"), lax.axis_index("row"), lax.axis_index("lev")
    peers = tiles * rows
    count = peers * levs
    me = (tile * rows + row) * levs + lev
    fields, owned, width = air_ref.shape
    slots = stripes_ref.shape[0]
    depth, lines = warm_ref.shape[:2]
    tables = area_ref.shape[0]
    picks = fields * slots
    places = peers * slots

    def device(o):
        return {"tile": o // (rows * levs), "row": (o // levs) % rows, "lev": o % levs}

    barrier = pltpu.get_barrier_semaphore()
    for j in range(1, count):
        pl.semaphore_signal(barrier, inc=1, device_id=device((me + j) % count), device_id_type=MESH)

    live = iota((slots, peers), 0) < tally_ref[...]
    listed = jnp.where(live, stripes_ref[...], -1)
    lane = iota((slots, peers * picks), 1)
    wide = jnp.zeros(lane.shape, jnp.int32)
    for d in range(peers):
        wide = jnp.where(lane // picks == d, listed[:, d : d + 1], wide)
    picked = jnp.sum(
        jnp.where(lane % slots == iota(lane.shape, 0), wide, 0), axis=0, keepdims=True
    )
    total = peers * picks
    at = iota((fields * owned, total), 0)
    to = iota((fields * owned, total), 1)
    chooser = jnp.where(
        jnp.logical_and(at // owned == (to // slots) % fields, at % owned == picked), 1.0, 0.0
    )
    chooser = chooser.T.astype(bf16)
    air_hi, air_lo = halves(air_ref[...].reshape(fields * owned, width))
    outbox[...] = (dot(chooser, air_hi) + dot(chooser, air_lo)).reshape(outbox.shape)

    sea = sea_ref[...].astype(f32)
    mix = mix_ref[...]
    edge[...] = jnp.zeros_like(edge)
    for side, line in ((0, 0), (1, lines - 1)):
        for l in range(depth):
            edge[side, l : l + 1, :] = warm_ref[l, line : line + 1, :]
        edge[side, depth : depth + 1, :] = sea[line : line + 1]
        edge[side, depth + 1 : depth + 2, :] = mix[line : line + 1]
    lane = iota((lines, width), 1)
    packed = jnp.zeros((lines, width), f32)
    for l in range(depth):
        packed = jnp.where(lane == l, warm_ref[l, :, 0:1], packed)
        packed = jnp.where(lane == depth + l, warm_ref[l, :, width - 1 : width], packed)
    packed = jnp.where(lane == 2 * depth, sea[:, 0:1], packed)
    packed = jnp.where(lane == 2 * depth + 1, sea[:, width - 1 : width], packed)
    packed = jnp.where(lane == 2 * depth + 2, mix[:, 0:1], packed)
    packed = jnp.where(lane == 2 * depth + 3, mix[:, width - 1 : width], packed)
    colbuf[...] = packed.T[: 3 * depth]

    pl.semaphore_wait(barrier, count - 1)

    def flux(j):
        o = (me + j) % count
        return pltpu.make_async_remote_copy(
            src_ref=outbox.at[o // levs],
            dst_ref=inbox.at[me],
            send_sem=flux_send.at[j],
            recv_sem=flux_recv.at[j],
            device_id=device(o),
            device_id_type=MESH,
        )

    for j in range(1, count):
        flux(j).start()
    inbox[pl.ds(me, 1)] = outbox[pl.ds(me // levs, 1)]

    halos = (
        (0, tile > 0, tile < tiles - 1, edge.at[0], zin.at[1], {"tile": jnp.maximum(tile - 1, 0)}),
        (1, tile < tiles - 1, tile > 0, edge.at[1], zin.at[0], {"tile": jnp.minimum(tile + 1, tiles - 1)}),
        (2, row > 0, row < rows - 1, colbuf, xin.at[1], {"row": jnp.maximum(row - 1, 0)}),
        (3, row < rows - 1, row > 0, colbuf, xin.at[0], {"row": jnp.minimum(row + 1, rows - 1)}),
    )

    def halo(i):
        n, there, comes, src, dst, target = halos[i]
        return pltpu.make_async_remote_copy(
            src_ref=src,
            dst_ref=dst,
            send_sem=halo_send.at[n],
            recv_sem=halo_recv.at[n],
            device_id=target,
            device_id_type=MESH,
        )

    for i in range(4):
        pl.when(halos[i][1])(lambda i=i: halo(i).start())

        @pl.when(jnp.logical_not(halos[i][2]))
        def _(i=i):
            halos[i][4][...] = jnp.zeros(halos[i][4].shape, f32)

    entry = iota((tables * places, lines), 0)
    counts = jnp.zeros((tables * places, lines), f32)
    for k in range(src_ref.shape[0]):
        ident = jnp.where(
            k < cnt_ref[...], wid_ref[k : k + 1, :] * places + src_ref[k : k + 1, :], -1
        )
        counts = counts + jnp.where(entry == ident, 1.0, 0.0)
    sel_t[...] = counts.astype(bf16)
    counts = counts.T.astype(bf16)
    sel[:, : tables * places] = counts
    sel[:, tables * places :] = counts

    for w in range(tables):
        hi, lo = halves(area_ref[w])
        area_cat[w * width : (w + 1) * width, :width] = hi
        area_cat[w * width : (w + 1) * width, width:] = lo
        hi, lo = halves(area_ref[w].T)
        area_t[0:width, w * width : (w + 1) * width] = hi
        area_t[width : 2 * width, w * width : (w + 1) * width] = lo

    ones = jnp.ones((places, 2 * width), bf16)
    sums = dot(ones, area_t[: 2 * width, :])
    for w in range(tables):
        hi, lo = halves(sums[:, w * width : (w + 1) * width])
        table[w * places : (w + 1) * places, :width] = hi
        table[(tables + w) * places : (tables + w + 1) * places, :width] = lo
    heat_scale = sea / dot(sel[...], table[:, :width])

    def backward(values):
        for w in range(tables):
            hi, lo = halves(values[w * places : (w + 1) * places])
            spread[:places, w * width : (w + 1) * width] = hi
            spread[places:, w * width : (w + 1) * width] = lo
        r = dot(spread[...], area_cat[...])
        return (r[:places, :width] + r[:places, width:]) + (r[places:, :width] + r[places:, width:])

    den = backward(dot(sel_t[...], sea.astype(bf16))) * (1.0 / levs)
    for p in range(peers):
        reply[p, slots : 2 * slots, :] = den[p * slots : (p + 1) * slots]

    size = peers * levs * picks
    by_level = jnp.where(iota((depth * places, depth), 0) // places == iota((depth * places, depth), 1), 1.0, 0.0)
    by_field = jnp.where(
        (iota((levs * fields, size), 1) // slots) % (levs * fields) == iota((levs * fields, size), 0), 1.0, 0.0
    )
    mixer = lax.dot_general(
        by_level, factor_ref[...], (((1,), (1,)), ((), ())), precision=precise, preferred_element_type=f32
    )
    mixer = jnp.dot(mixer, by_field, precision=precise, preferred_element_type=f32)
    r = iota((depth * places, size), 0)
    c = iota((depth * places, size), 1)
    same = jnp.logical_and((r // slots) % peers == c // (levs * picks), r % slots == c % slots)
    mix_hi, mix_lo = halves(jnp.where(same, mixer, 0.0))

    right = 0.5 * (mix + pltpu.roll(mix, width - 1, 1)) * sea * pltpu.roll(sea, width - 1, 1)
    right = jnp.where(lane == width - 1, 0.0, right)
    line = iota((lines, width), 0)
    down = 0.5 * (mix + pltpu.roll(mix, lines - 1, 0)) * sea * pltpu.roll(sea, lines - 1, 0)
    down = jnp.where(line == lines - 1, 0.0, down)
    for i in range(4):
        pl.when(halos[i][2])(lambda i=i: halo(i).wait_recv())
    side = []
    for n, edge_line in ((0, 0), (1, lines - 1)):
        coef = (
            edge[n, depth : depth + 1, :] * zin[n, depth : depth + 1, :] * 0.5
            * (edge[n, depth + 1 : depth + 2, :] + zin[n, depth + 1 : depth + 2, :])
        )
        side.append(coef * (zin[n, :depth, :] - edge[n, :depth, :]))
    dbuf[...] = jnp.zeros_like(dbuf)
    for n in range(2):
        o = 1 - n
        coef = (
            colbuf[2 * depth + n : 2 * depth + n + 1, :]
            * xin[n, 2 * depth + o : 2 * depth + o + 1, :]
            * 0.5
            * (
                colbuf[2 * depth + 2 + n : 2 * depth + 3 + n, :]
                + xin[n, 2 * depth + 2 + o : 2 * depth + 3 + o, :]
            )
        )
        dbuf[n * depth : (n + 1) * depth, :] = coef * (
            xin[n, o * depth : (o + 1) * depth, :] - colbuf[n * depth : (n + 1) * depth, :]
        )
    columns = dbuf[...].T
    for l in range(depth):
        heat = warm_ref[l]
        east = right * (pltpu.roll(heat, width - 1, 1) - heat)
        south = down * (pltpu.roll(heat, lines - 1, 0) - heat)
        moved = heat + ((east - pltpu.roll(east, 1, 1)) + (south - pltpu.roll(south, 1, 0)))
        moved = moved + jnp.where(lane == 0, columns[:, l : l + 1], 0.0)
        moved = moved + jnp.where(lane == width - 1, columns[:, depth + l : depth + l + 1], 0.0)
        moved = moved + jnp.where(line == 0, side[0][l : l + 1], 0.0)
        base[l] = moved + jnp.where(line == lines - 1, side[1][l : l + 1], 0.0)

    for j in range(1, count):
        flux(j).wait_recv()
    got_hi, got_lo = halves(inbox[...].reshape(size, width))
    level_flux = dot(mix_hi, got_hi) + (dot(mix_hi, got_lo) + dot(mix_lo, got_hi))
    g_hi, g_lo = halves(level_flux)
    for w in range(0, tables, 2):
        at = slice(w * width, (w + 2) * width)
        part = dot(g_hi, area_t[:width, at]) + (
            dot(g_hi, area_t[width : 2 * width, at]) + dot(g_lo, area_t[:width, at])
        )
        hi, lo = halves(part)
        for n in range(2):
            for l in range(depth):
                put = slice((w + n) * places, (w + n + 1) * places)
                put_lo = slice((tables + w + n) * places, (tables + w + n + 1) * places)
                rows_l = slice(l * places, (l + 1) * places)
                cols_l = slice(n * width, (n + 1) * width)
                table[put, l * width : (l + 1) * width] = hi[rows_l, cols_l]
                table[put_lo, l * width : (l + 1) * width] = lo[rows_l, cols_l]
    thick_sum = thick_ref[0]
    for l in range(1, levs * depth):
        thick_sum = thick_sum + thick_ref[l]
    surface = jnp.zeros((lines, width), f32)
    for l in range(0, depth, 2):
        heating = dot(sel[...], table[:, l * width : (l + 2) * width])
        for n in range(2):
            heat = base[l + n] + heat_scale * heating[:, n * width : (n + 1) * width]
            out_ref[l + n] = heat
            surface = surface + thick_ref[lev * depth + l + n] * heat
    surface = sea * surface / thick_sum

    hi, lo = halves(surface)
    num = backward(dot(sel_t[...], hi) + dot(sel_t[...], lo))
    for p in range(peers):
        reply[p, :slots, :] = num[p * slots : (p + 1) * slots]

    def back(j):
        o = (me + j) % count
        return pltpu.make_async_remote_copy(
            src_ref=reply.at[o // levs],
            dst_ref=replies.at[me],
            send_sem=back_send.at[j],
            recv_sem=back_recv.at[j],
            device_id=device(o),
            device_id_type=MESH,
        )

    for j in range(1, count):
        back(j).start()
    replies[pl.ds(me, 1)] = reply[pl.ds(me // levs, 1)]
    at = iota((2 * owned, total), 0)
    to = iota((2 * owned, total), 1)
    gather = jnp.where(
        jnp.logical_and(at % owned == picked, at // owned == (to % (2 * slots)) // slots), 1.0, 0.0
    ).astype(bf16)
    for j in range(1, count):
        back(j).wait_recv()
    hi, lo = halves(replies[...].reshape(total, width))
    sums = dot(gather, hi) + dot(gather, lo)
    skin_ref[...] = sums[:owned] / jnp.maximum(sums[owned:], 1.0)

    for j in range(1, count):
        flux(j).wait_send()
        back(j).wait_send()
    for i in range(4):
        pl.when(halos[i][1])(lambda i=i: halo(i).wait_send())


def fused(
    tiles, rows, levs,
    air_exchange_rates, outgoing_stripes, outgoing_tally, regrid_inputs, regrid_factor_id,
    regrid_tally, intersection_areas, sea_indicator, mixing_rate, warmth_profile,
    warming_factor, stratum_depths,
):
    fields, owned, width = air_exchange_rates.shape
    slots = outgoing_stripes.shape[2]
    depth, lines = warmth_profile.shape[:2]
    tables = intersection_areas.shape[0]
    peers = tiles * rows
    count = peers * levs
    places = peers * slots
    vmem = pl.BlockSpec(memory_space=pltpu.VMEM)
    smem = pl.BlockSpec(memory_space=pltpu.SMEM)
    dma = pltpu.SemaphoreType.DMA
    return pl.pallas_call(
        functools.partial(window, tiles, rows, levs),
        out_shape=(
            jax.ShapeDtypeStruct(warmth_profile.shape, f32),
            jax.ShapeDtypeStruct((owned, width), f32),
        ),
        in_specs=[vmem] * 11 + [smem],
        out_specs=(vmem, vmem),
        scratch_shapes=[
            pltpu.VMEM((peers, fields * slots, width), f32),
            pltpu.VMEM((count, fields * slots, width), f32),
            pltpu.VMEM((2, 2 * depth, width), f32),
            pltpu.VMEM((2, 2 * depth, width), f32),
            pltpu.VMEM((3 * depth, lines), f32),
            pltpu.VMEM((2, 3 * depth, lines), f32),
            pltpu.VMEM((width, lines), f32),
            pltpu.VMEM((lines, 2 * tables * places), bf16),
            pltpu.VMEM((tables * places, lines), bf16),
            pltpu.VMEM((2 * width, tables * width), bf16),
            pltpu.VMEM((tables * width, 2 * width), bf16),
            pltpu.VMEM((2 * tables * places, depth * width), bf16),
            pltpu.VMEM((depth, lines, width), f32),
            pltpu.VMEM((2 * places, tables * width), bf16),
            pltpu.VMEM((peers, 2 * slots, width), f32),
            pltpu.VMEM((count, 2 * slots, width), f32),
            dma((count,)), dma((count,)), dma((4,)), dma((4,)), dma((count,)), dma((count,)),
        ],
        compiler_params=pltpu.CompilerParams(
            collective_id=0, has_side_effects=True, vmem_limit_bytes=48 * 1024 * 1024
        ),
        name="window",
    )(
        air_exchange_rates,
        outgoing_stripes[0].T,
        outgoing_tally,
        regrid_inputs[:, 0, :].T,
        regrid_factor_id[:, 0, :].T,
        regrid_tally.T,
        intersection_areas,
        sea_indicator,
        mixing_rate,
        warmth_profile,
        warming_factor,
        stratum_depths,
    )


def extended(cells, sides, width):
    for axis, dim in sides:
        count = lax.axis_size(axis)
        ends = count - 1
        head = lax.slice_in_dim(cells, 0, width, axis=dim)
        tail = lax.slice_in_dim(cells, cells.shape[dim] - width, cells.shape[dim], axis=dim)
        cells = jnp.concatenate(
            [
                lax.ppermute(tail, axis, [(i, (i + 1) % count) for i in range(ends)]),
                cells,
                lax.ppermute(head, axis, [((i + 1) % count, i) for i in range(ends)]),
            ],
            axis=dim,
        )
    return cells


def shards(
    air_exchange_rates,
    outgoing_stripes,
    outgoing_tally,
    regrid_inputs,
    regrid_factor_id,
    regrid_tally,
    intersection_areas,
    sea_indicator,
    mixing_rate,
    warmth_profile,
    warming_factor,
    stratum_depths,
):
    tile_count = lax.axis_size("tile")
    row_count = lax.axis_size("row")
    peer_count = tile_count * row_count
    field_count, atm_rows, width = air_exchange_rates.shape
    slot_count = outgoing_stripes.shape[2]
    marine_stripes = warmth_profile.shape[1]
    depth_tally = warmth_profile.shape[0]
    block_most = regrid_inputs.shape[2]
    table_size = intersection_areas.shape[0]
    row_list = outgoing_stripes[0].reshape(-1)
    live_slot = (
        (jnp.arange(slot_count, dtype=jnp.int32)[None, :] < outgoing_tally[0][:, None])
        .reshape(-1)
        .astype(jnp.float32)
    )
    picker = (row_list[:, None] == jnp.arange(atm_rows, dtype=jnp.int32)[None, :]).astype(
        jnp.float32
    ) * live_slot[:, None]
    outgoing = jnp.einsum("qa,fac->qfc", picker, air_exchange_rates, precision=precise)
    arrived = lax.all_to_all(outgoing, ("tile", "row"), split_axis=0, concat_axis=0, tiled=True)
    source_slot = regrid_inputs[:, 0, :]
    weight_id = regrid_factor_id[:, 0, :]
    block_count = regrid_tally[:, 0]
    usable = (jnp.arange(block_most, dtype=jnp.int32)[None, :] < block_count[:, None]).astype(
        jnp.float32
    )
    selector = (
        weight_id[:, :, None] == jnp.arange(table_size, dtype=jnp.int32)[None, None, :]
    ).astype(jnp.float32) * usable[:, :, None]
    fetched = arrived[source_slot]
    grouped = jnp.einsum("xkw,xkfc->wxfc", selector, fetched, precision=precise)
    summed = jnp.einsum("wec,wxfc->fxe", intersection_areas, grouped, precision=precise)
    coverage = jnp.einsum(
        "xkw,we->xe", selector, jnp.sum(intersection_areas, axis=2), precision=precise
    )
    local_flux = summed / coverage[None]
    all_flux = lax.all_gather(local_flux, "lev", axis=0, tiled=True)
    thermal_tendency = jnp.einsum("fl,fxc->lxc", warming_factor, all_flux, precision=precise)
    marine_indicator = sea_indicator.astype(jnp.float32)
    piled_arrays = jnp.concatenate(
        [warmth_profile, marine_indicator[None], mixing_rate[None]], axis=0
    )
    padded = extended(piled_arrays, (("tile", 1), ("row", 2)), 1)
    spread_tracer = jnp.zeros_like(warmth_profile)
    for step_x, step_y in ((1, 0), (-1, 0), (0, 1), (0, -1)):
        neighbour_values = padded[
            :, 1 + step_x : 1 + step_x + marine_stripes, 1 + step_y : 1 + step_y + width
        ]
        spread_tracer = spread_tracer + neighbour_values[depth_tally] * 0.5 * (
            mixing_rate + neighbour_values[depth_tally + 1]
        ) * (neighbour_values[:depth_tally] - warmth_profile)
    warmth_following = warmth_profile + marine_indicator * (spread_tracer + thermal_tendency)
    level_start = lax.axis_index("lev") * depth_tally
    own_thick = lax.dynamic_slice_in_dim(stratum_depths, level_start, depth_tally)
    partial_value = jnp.einsum(
        "l,lxc->xc", own_thick, warmth_following, precision=precise
    ) / jnp.sum(stratum_depths)
    topmost_stratum = lax.psum(partial_value, "lev")
    columns = intersection_areas.shape[2]
    coupled_entries = jnp.stack([marine_indicator * topmost_stratum, marine_indicator], axis=1)
    spread = jnp.einsum("wec,xje->wxjc", intersection_areas, coupled_entries, precision=precise)
    contribution = jnp.einsum("xkw,wxjc->xkjc", selector, spread, precision=precise)
    target = (
        source_slot.reshape(-1)[:, None]
        == jnp.arange(peer_count * slot_count, dtype=jnp.int32)[None, :]
    ).astype(jnp.float32)
    returning = jnp.einsum(
        "rq,rjc->qjc",
        target,
        contribution.reshape(marine_stripes * block_most, 2, columns),
        precision=precise,
    )
    returned = lax.all_to_all(
        returning.reshape(peer_count, slot_count, 2, columns),
        ("tile", "row"),
        split_axis=0,
        concat_axis=0,
        tiled=True,
    )
    returned = returned.reshape(peer_count * slot_count, 2, columns)
    atm_sums = jnp.einsum("qa,qjc->ajc", picker, returned, precision=precise)
    dividend_sum = atm_sums[:, 0]
    divisor_sum = atm_sums[:, 1]
    air_side_skin_heat = dividend_sum / jnp.maximum(divisor_sum, 1.0)
    return (warmth_following, air_side_skin_heat)


def solution(mesh):
    placed = (
        P("lev", ("groups", "tile", "row"), None),
        P(("groups", "tile", "row"), None, None),
        P(("groups", "tile", "row"), None),
        P(("groups", "tile"), "row", None),
        P(("groups", "tile"), "row", None),
        P(("groups", "tile"), "row"),
        P("groups", None, None),
        P(("groups", "tile"), "row"),
        P(("groups", "tile"), "row"),
        P("lev", ("groups", "tile"), "row"),
        P(None, "lev"),
        P(),
    )
    tiles, rows, levs = mesh.shape["tile"], mesh.shape["row"], mesh.shape["lev"]
    small = tiles * rows * levs <= SMALL and levs == 2
    return jax.shard_map(
        functools.partial(fused, tiles, rows, levs) if small else shards,
        mesh=mesh,
        in_specs=placed,
        out_specs=(P("lev", ("groups", "tile"), "row"), P(("groups", "tile", "row"), None)),
        check_vma=False,
    )
```

```python
import functools
import jax
import jax.numpy as jnp
from jax import lax
from jax.experimental import pallas as pl
from jax.experimental.pallas import tpu as pltpu
from jax.sharding import PartitionSpec as P

precise = lax.Precision.HIGHEST
f32 = jnp.float32
bf16 = jnp.bfloat16
MESH = pl.DeviceIdType.MESH
FIRST, SECOND, THIRD = (1, 2, 0), (7, 8, 9), (3, 4, 5, 6, 10, 11)
SMALL = 16


def halves(v):
    hi = v.astype(bf16)
    return hi, (v - hi.astype(f32)).astype(bf16)


def iota(shape, dim):
    return lax.broadcasted_iota(jnp.int32, shape, dim)


def dot(a, b):
    return jnp.dot(a, b, preferred_element_type=f32)


def window(
    tiles, rows, levs,
    *refs,
):
    sources, (out_ref, skin_ref), held = refs[:12], refs[12:14], refs[14:26]
    loads = [
        pltpu.make_async_copy(source, target, refs[-1].at[n])
        for n, (source, target) in enumerate(zip(sources, held))
    ]
    for n in FIRST + SECOND + THIRD:
        loads[n].start()
    exchange(tiles, rows, levs, loads, *held, out_ref, skin_ref, *refs[26:-1])


def exchange(
    tiles, rows, levs, loads,
    air_ref, stripes_ref, tally_ref, src_ref, wid_ref, cnt_ref, area_ref, sea_ref, mix_ref,
    warm_ref, factor_ref, thick_ref,
    out_ref, skin_ref,
    outbox, inbox, edge, zin, colbuf, xin, dbuf, sel, sel_t, area_t, area_cat, table, base,
    spread, reply, replies,
    flux_send, flux_recv, halo_send, halo_recv, back_send, back_recv,
):
    tile, row, lev = lax.axis_index("tile"), lax.axis_index("row"), lax.axis_index("lev")
    peers = tiles * rows
    count = peers * levs
    me = (tile * rows + row) * levs + lev
    fields, owned, width = air_ref.shape
    slots = stripes_ref.shape[0]
    depth, lines = warm_ref.shape[:2]
    tables = area_ref.shape[0]
    picks = fields * slots
    places = peers * slots

    def device(o):
        return {"tile": o // (rows * levs), "row": (o // levs) % rows, "lev": o % levs}

    barrier = pltpu.get_barrier_semaphore()
    for j in range(1, count):
        pl.semaphore_signal(barrier, inc=1, device_id=device((me + j) % count), device_id_type=MESH)

    for n in FIRST:
        loads[n].wait()

    live = iota((slots, peers), 0) < tally_ref[...]
    listed = jnp.where(live, stripes_ref[...], -1)
    lane = iota((slots, peers * picks), 1)
    wide = jnp.zeros(lane.shape, jnp.int32)
    for d in range(peers):
        wide = jnp.where(lane // picks == d, listed[:, d : d + 1], wide)
    picked = jnp.sum(
        jnp.where(lane % slots == iota(lane.shape, 0), wide, 0), axis=0, keepdims=True
    )
    total = peers * picks
    at = iota((fields * owned, total), 0)
    to = iota((fields * owned, total), 1)
    chooser = jnp.where(
        jnp.logical_and(at // owned == (to // slots) % fields, at % owned == picked), 1.0, 0.0
    )
    chooser = chooser.T.astype(bf16)
    air_hi, air_lo = halves(air_ref[...].reshape(fields * owned, width))
    outbox[...] = (dot(chooser, air_hi) + dot(chooser, air_lo)).reshape(outbox.shape)

    for n in SECOND:
        loads[n].wait()
    sea = sea_ref[...].astype(f32)
    mix = mix_ref[...]
    edge[...] = jnp.zeros_like(edge)
    for side, line in ((0, 0), (1, lines - 1)):
        for l in range(depth):
            edge[side, l : l + 1, :] = warm_ref[l, line : line + 1, :]
        edge[side, depth : depth + 1, :] = sea[line : line + 1]
        edge[side, depth + 1 : depth + 2, :] = mix[line : line + 1]
    lane = iota((lines, width), 1)
    packed = jnp.zeros((lines, width), f32)
    for l in range(depth):
        packed = jnp.where(lane == l, warm_ref[l, :, 0:1], packed)
        packed = jnp.where(lane == depth + l, warm_ref[l, :, width - 1 : width], packed)
    packed = jnp.where(lane == 2 * depth, sea[:, 0:1], packed)
    packed = jnp.where(lane == 2 * depth + 1, sea[:, width - 1 : width], packed)
    packed = jnp.where(lane == 2 * depth + 2, mix[:, 0:1], packed)
    packed = jnp.where(lane == 2 * depth + 3, mix[:, width - 1 : width], packed)
    colbuf[...] = packed.T[: 3 * depth]

    pl.semaphore_wait(barrier, count - 1)

    def flux(j):
        o = (me + j) % count
        return pltpu.make_async_remote_copy(
            src_ref=outbox.at[o // levs],
            dst_ref=inbox.at[me],
            send_sem=flux_send.at[j],
            recv_sem=flux_recv.at[j],
            device_id=device(o),
            device_id_type=MESH,
        )

    for j in range(1, count):
        flux(j).start()
    inbox[pl.ds(me, 1)] = outbox[pl.ds(me // levs, 1)]

    halos = (
        (0, tile > 0, tile < tiles - 1, edge.at[0], zin.at[1], {"tile": jnp.maximum(tile - 1, 0)}),
        (1, tile < tiles - 1, tile > 0, edge.at[1], zin.at[0], {"tile": jnp.minimum(tile + 1, tiles - 1)}),
        (2, row > 0, row < rows - 1, colbuf, xin.at[1], {"row": jnp.maximum(row - 1, 0)}),
        (3, row < rows - 1, row > 0, colbuf, xin.at[0], {"row": jnp.minimum(row + 1, rows - 1)}),
    )

    def halo(i):
        n, there, comes, src, dst, target = halos[i]
        return pltpu.make_async_remote_copy(
            src_ref=src,
            dst_ref=dst,
            send_sem=halo_send.at[n],
            recv_sem=halo_recv.at[n],
            device_id=target,
            device_id_type=MESH,
        )

    for i in range(4):
        pl.when(halos[i][1])(lambda i=i: halo(i).start())

        @pl.when(jnp.logical_not(halos[i][2]))
        def _(i=i):
            halos[i][4][...] = jnp.zeros(halos[i][4].shape, f32)

    for n in THIRD:
        loads[n].wait()

    entry = iota((tables * places, lines), 0)
    counts = jnp.zeros((tables * places, lines), f32)
    for k in range(src_ref.shape[0]):
        ident = jnp.where(
            k < cnt_ref[...], wid_ref[k : k + 1, :] * places + src_ref[k : k + 1, :], -1
        )
        counts = counts + jnp.where(entry == ident, 1.0, 0.0)
    sel_t[...] = counts.astype(bf16)
    counts = counts.T.astype(bf16)
    sel[:, : tables * places] = counts
    sel[:, tables * places :] = counts

    for w in range(tables):
        hi, lo = halves(area_ref[w])
        area_cat[w * width : (w + 1) * width, :width] = hi
        area_cat[w * width : (w + 1) * width, width:] = lo
        hi, lo = halves(area_ref[w].T)
        area_t[0:width, w * width : (w + 1) * width] = hi
        area_t[width : 2 * width, w * width : (w + 1) * width] = lo

    ones = jnp.ones((places, 2 * width), bf16)
    sums = dot(ones, area_t[: 2 * width, :])
    for w in range(tables):
        hi, lo = halves(sums[:, w * width : (w + 1) * width])
        table[w * places : (w + 1) * places, :width] = hi
        table[(tables + w) * places : (tables + w + 1) * places, :width] = lo
    heat_scale = sea / dot(sel[...], table[:, :width])

    def backward(values):
        for w in range(tables):
            hi, lo = halves(values[w * places : (w + 1) * places])
            spread[:places, w * width : (w + 1) * width] = hi
            spread[places:, w * width : (w + 1) * width] = lo
        r = dot(spread[...], area_cat[...])
        return (r[:places, :width] + r[:places, width:]) + (r[places:, :width] + r[places:, width:])

    den = backward(dot(sel_t[...], sea.astype(bf16))) * (1.0 / levs)
    for p in range(peers):
        reply[p, slots : 2 * slots, :] = den[p * slots : (p + 1) * slots]

    size = peers * levs * picks
    by_level = jnp.where(iota((depth * places, depth), 0) // places == iota((depth * places, depth), 1), 1.0, 0.0)
    by_field = jnp.where(
        (iota((levs * fields, size), 1) // slots) % (levs * fields) == iota((levs * fields, size), 0), 1.0, 0.0
    )
    mixer = lax.dot_general(
        by_level, factor_ref[...], (((1,), (1,)), ((), ())), precision=precise, preferred_element_type=f32
    )
    mixer = jnp.dot(mixer, by_field, precision=precise, preferred_element_type=f32)
    r = iota((depth * places, size), 0)
    c = iota((depth * places, size), 1)
    same = jnp.logical_and((r // slots) % peers == c // (levs * picks), r % slots == c % slots)
    mix_hi, mix_lo = halves(jnp.where(same, mixer, 0.0))

    right = 0.5 * (mix + pltpu.roll(mix, width - 1, 1)) * sea * pltpu.roll(sea, width - 1, 1)
    right = jnp.where(lane == width - 1, 0.0, right)
    line = iota((lines, width), 0)
    down = 0.5 * (mix + pltpu.roll(mix, lines - 1, 0)) * sea * pltpu.roll(sea, lines - 1, 0)
    down = jnp.where(line == lines - 1, 0.0, down)
    for i in range(4):
        pl.when(halos[i][2])(lambda i=i: halo(i).wait_recv())
    side = []
    for n, edge_line in ((0, 0), (1, lines - 1)):
        coef = (
            edge[n, depth : depth + 1, :] * zin[n, depth : depth + 1, :] * 0.5
            * (edge[n, depth + 1 : depth + 2, :] + zin[n, depth + 1 : depth + 2, :])
        )
        side.append(coef * (zin[n, :depth, :] - edge[n, :depth, :]))
    dbuf[...] = jnp.zeros_like(dbuf)
    for n in range(2):
        o = 1 - n
        coef = (
            colbuf[2 * depth + n : 2 * depth + n + 1, :]
            * xin[n, 2 * depth + o : 2 * depth + o + 1, :]
            * 0.5
            * (
                colbuf[2 * depth + 2 + n : 2 * depth + 3 + n, :]
                + xin[n, 2 * depth + 2 + o : 2 * depth + 3 + o, :]
            )
        )
        dbuf[n * depth : (n + 1) * depth, :] = coef * (
            xin[n, o * depth : (o + 1) * depth, :] - colbuf[n * depth : (n + 1) * depth, :]
        )
    columns = dbuf[...].T
    for l in range(depth):
        heat = warm_ref[l]
        east = right * (pltpu.roll(heat, width - 1, 1) - heat)
        south = down * (pltpu.roll(heat, lines - 1, 0) - heat)
        moved = heat + ((east - pltpu.roll(east, 1, 1)) + (south - pltpu.roll(south, 1, 0)))
        moved = moved + jnp.where(lane == 0, columns[:, l : l + 1], 0.0)
        moved = moved + jnp.where(lane == width - 1, columns[:, depth + l : depth + l + 1], 0.0)
        moved = moved + jnp.where(line == 0, side[0][l : l + 1], 0.0)
        base[l] = moved + jnp.where(line == lines - 1, side[1][l : l + 1], 0.0)

    for j in range(1, count):
        flux(j).wait_recv()
    got_hi, got_lo = halves(inbox[...].reshape(size, width))
    level_flux = dot(mix_hi, got_hi) + (dot(mix_hi, got_lo) + dot(mix_lo, got_hi))
    g_hi, g_lo = halves(level_flux)
    for w in range(0, tables, 2):
        at = slice(w * width, (w + 2) * width)
        part = dot(g_hi, area_t[:width, at]) + (
            dot(g_hi, area_t[width : 2 * width, at]) + dot(g_lo, area_t[:width, at])
        )
        hi, lo = halves(part)
        for n in range(2):
            for l in range(depth):
                put = slice((w + n) * places, (w + n + 1) * places)
                put_lo = slice((tables + w + n) * places, (tables + w + n + 1) * places)
                rows_l = slice(l * places, (l + 1) * places)
                cols_l = slice(n * width, (n + 1) * width)
                table[put, l * width : (l + 1) * width] = hi[rows_l, cols_l]
                table[put_lo, l * width : (l + 1) * width] = lo[rows_l, cols_l]
    thick_sum = thick_ref[0]
    for l in range(1, levs * depth):
        thick_sum = thick_sum + thick_ref[l]
    surface = jnp.zeros((lines, width), f32)
    for l in range(0, depth, 2):
        heating = dot(sel[...], table[:, l * width : (l + 2) * width])
        for n in range(2):
            heat = base[l + n] + heat_scale * heating[:, n * width : (n + 1) * width]
            out_ref[l + n] = heat
            surface = surface + thick_ref[lev * depth + l + n] * heat
    surface = sea * surface / thick_sum

    hi, lo = halves(surface)
    num = backward(dot(sel_t[...], hi) + dot(sel_t[...], lo))
    for p in range(peers):
        reply[p, :slots, :] = num[p * slots : (p + 1) * slots]

    def back(j):
        o = (me + j) % count
        return pltpu.make_async_remote_copy(
            src_ref=reply.at[o // levs],
            dst_ref=replies.at[me],
            send_sem=back_send.at[j],
            recv_sem=back_recv.at[j],
            device_id=device(o),
            device_id_type=MESH,
        )

    for j in range(1, count):
        back(j).start()
    replies[pl.ds(me, 1)] = reply[pl.ds(me // levs, 1)]
    at = iota((2 * owned, total), 0)
    to = iota((2 * owned, total), 1)
    gather = jnp.where(
        jnp.logical_and(at % owned == picked, at // owned == (to % (2 * slots)) // slots), 1.0, 0.0
    ).astype(bf16)
    for j in range(1, count):
        back(j).wait_recv()
    hi, lo = halves(replies[...].reshape(total, width))
    sums = dot(gather, hi) + dot(gather, lo)
    skin_ref[...] = sums[:owned] / jnp.maximum(sums[owned:], 1.0)

    for j in range(1, count):
        flux(j).wait_send()
        back(j).wait_send()
    for i in range(4):
        pl.when(halos[i][1])(lambda i=i: halo(i).wait_send())


def fused(
    tiles, rows, levs,
    air_exchange_rates, outgoing_stripes, outgoing_tally, regrid_inputs, regrid_factor_id,
    regrid_tally, intersection_areas, sea_indicator, mixing_rate, warmth_profile,
    warming_factor, stratum_depths,
):
    fields, owned, width = air_exchange_rates.shape
    slots = outgoing_stripes.shape[2]
    depth, lines = warmth_profile.shape[:2]
    tables = intersection_areas.shape[0]
    peers = tiles * rows
    count = peers * levs
    places = peers * slots
    vmem = pl.BlockSpec(memory_space=pltpu.VMEM)
    operands = (
        air_exchange_rates,
        outgoing_stripes[0].T,
        outgoing_tally,
        regrid_inputs[:, 0, :].T,
        regrid_factor_id[:, 0, :].T,
        regrid_tally.T,
        intersection_areas,
        sea_indicator,
        mixing_rate,
        warmth_profile,
        warming_factor,
        stratum_depths,
    )
    dma = pltpu.SemaphoreType.DMA
    return pl.pallas_call(
        functools.partial(window, tiles, rows, levs),
        out_shape=(
            jax.ShapeDtypeStruct(warmth_profile.shape, f32),
            jax.ShapeDtypeStruct((owned, width), f32),
        ),
        in_specs=[pl.BlockSpec(memory_space=pltpu.HBM)] * 12,
        out_specs=(vmem, vmem),
        scratch_shapes=[pltpu.VMEM(x.shape, x.dtype) for x in operands[:11]]
        + [pltpu.SMEM(stratum_depths.shape, f32)]
        + [
            pltpu.VMEM((peers, fields * slots, width), f32),
            pltpu.VMEM((count, fields * slots, width), f32),
            pltpu.VMEM((2, 2 * depth, width), f32),
            pltpu.VMEM((2, 2 * depth, width), f32),
            pltpu.VMEM((3 * depth, lines), f32),
            pltpu.VMEM((2, 3 * depth, lines), f32),
            pltpu.VMEM((width, lines), f32),
            pltpu.VMEM((lines, 2 * tables * places), bf16),
            pltpu.VMEM((tables * places, lines), bf16),
            pltpu.VMEM((2 * width, tables * width), bf16),
            pltpu.VMEM((tables * width, 2 * width), bf16),
            pltpu.VMEM((2 * tables * places, depth * width), bf16),
            pltpu.VMEM((depth, lines, width), f32),
            pltpu.VMEM((2 * places, tables * width), bf16),
            pltpu.VMEM((peers, 2 * slots, width), f32),
            pltpu.VMEM((count, 2 * slots, width), f32),
            dma((count,)), dma((count,)), dma((4,)), dma((4,)), dma((count,)), dma((count,)),
            dma((12,)),
        ],
        compiler_params=pltpu.CompilerParams(
            collective_id=0, has_side_effects=True, vmem_limit_bytes=60 * 1024 * 1024
        ),
        name="window",
    )(*operands)


def extended(cells, sides, width):
    for axis, dim in sides:
        count = lax.axis_size(axis)
        ends = count - 1
        head = lax.slice_in_dim(cells, 0, width, axis=dim)
        tail = lax.slice_in_dim(cells, cells.shape[dim] - width, cells.shape[dim], axis=dim)
        cells = jnp.concatenate(
            [
                lax.ppermute(tail, axis, [(i, (i + 1) % count) for i in range(ends)]),
                cells,
                lax.ppermute(head, axis, [((i + 1) % count, i) for i in range(ends)]),
            ],
            axis=dim,
        )
    return cells


def shards(
    air_exchange_rates,
    outgoing_stripes,
    outgoing_tally,
    regrid_inputs,
    regrid_factor_id,
    regrid_tally,
    intersection_areas,
    sea_indicator,
    mixing_rate,
    warmth_profile,
    warming_factor,
    stratum_depths,
):
    tile_count = lax.axis_size("tile")
    row_count = lax.axis_size("row")
    peer_count = tile_count * row_count
    field_count, atm_rows, width = air_exchange_rates.shape
    slot_count = outgoing_stripes.shape[2]
    marine_stripes = warmth_profile.shape[1]
    depth_tally = warmth_profile.shape[0]
    block_most = regrid_inputs.shape[2]
    table_size = intersection_areas.shape[0]
    row_list = outgoing_stripes[0].reshape(-1)
    live_slot = (
        (jnp.arange(slot_count, dtype=jnp.int32)[None, :] < outgoing_tally[0][:, None])
        .reshape(-1)
        .astype(jnp.float32)
    )
    picker = (row_list[:, None] == jnp.arange(atm_rows, dtype=jnp.int32)[None, :]).astype(
        jnp.float32
    ) * live_slot[:, None]
    outgoing = jnp.einsum("qa,fac->qfc", picker, air_exchange_rates, precision=precise)
    arrived = lax.all_to_all(outgoing, ("tile", "row"), split_axis=0, concat_axis=0, tiled=True)
    source_slot = regrid_inputs[:, 0, :]
    weight_id = regrid_factor_id[:, 0, :]
    block_count = regrid_tally[:, 0]
    usable = (jnp.arange(block_most, dtype=jnp.int32)[None, :] < block_count[:, None]).astype(
        jnp.float32
    )
    selector = (
        weight_id[:, :, None] == jnp.arange(table_size, dtype=jnp.int32)[None, None, :]
    ).astype(jnp.float32) * usable[:, :, None]
    fetched = arrived[source_slot]
    grouped = jnp.einsum("xkw,xkfc->wxfc", selector, fetched, precision=precise)
    summed = jnp.einsum("wec,wxfc->fxe", intersection_areas, grouped, precision=precise)
    coverage = jnp.einsum(
        "xkw,we->xe", selector, jnp.sum(intersection_areas, axis=2), precision=precise
    )
    local_flux = summed / coverage[None]
    all_flux = lax.all_gather(local_flux, "lev", axis=0, tiled=True)
    thermal_tendency = jnp.einsum("fl,fxc->lxc", warming_factor, all_flux, precision=precise)
    marine_indicator = sea_indicator.astype(jnp.float32)
    piled_arrays = jnp.concatenate(
        [warmth_profile, marine_indicator[None], mixing_rate[None]], axis=0
    )
    padded = extended(piled_arrays, (("tile", 1), ("row", 2)), 1)
    spread_tracer = jnp.zeros_like(warmth_profile)
    for step_x, step_y in ((1, 0), (-1, 0), (0, 1), (0, -1)):
        neighbour_values = padded[
            :, 1 + step_x : 1 + step_x + marine_stripes, 1 + step_y : 1 + step_y + width
        ]
        spread_tracer = spread_tracer + neighbour_values[depth_tally] * 0.5 * (
            mixing_rate + neighbour_values[depth_tally + 1]
        ) * (neighbour_values[:depth_tally] - warmth_profile)
    warmth_following = warmth_profile + marine_indicator * (spread_tracer + thermal_tendency)
    level_start = lax.axis_index("lev") * depth_tally
    own_thick = lax.dynamic_slice_in_dim(stratum_depths, level_start, depth_tally)
    partial_value = jnp.einsum(
        "l,lxc->xc", own_thick, warmth_following, precision=precise
    ) / jnp.sum(stratum_depths)
    topmost_stratum = lax.psum(partial_value, "lev")
    columns = intersection_areas.shape[2]
    coupled_entries = jnp.stack([marine_indicator * topmost_stratum, marine_indicator], axis=1)
    spread = jnp.einsum("wec,xje->wxjc", intersection_areas, coupled_entries, precision=precise)
    contribution = jnp.einsum("xkw,wxjc->xkjc", selector, spread, precision=precise)
    target = (
        source_slot.reshape(-1)[:, None]
        == jnp.arange(peer_count * slot_count, dtype=jnp.int32)[None, :]
    ).astype(jnp.float32)
    returning = jnp.einsum(
        "rq,rjc->qjc",
        target,
        contribution.reshape(marine_stripes * block_most, 2, columns),
        precision=precise,
    )
    returned = lax.all_to_all(
        returning.reshape(peer_count, slot_count, 2, columns),
        ("tile", "row"),
        split_axis=0,
        concat_axis=0,
        tiled=True,
    )
    returned = returned.reshape(peer_count * slot_count, 2, columns)
    atm_sums = jnp.einsum("qa,qjc->ajc", picker, returned, precision=precise)
    dividend_sum = atm_sums[:, 0]
    divisor_sum = atm_sums[:, 1]
    air_side_skin_heat = dividend_sum / jnp.maximum(divisor_sum, 1.0)
    return (warmth_following, air_side_skin_heat)


def solution(mesh):
    placed = (
        P("lev", ("groups", "tile", "row"), None),
        P(("groups", "tile", "row"), None, None),
        P(("groups", "tile", "row"), None),
        P(("groups", "tile"), "row", None),
        P(("groups", "tile"), "row", None),
        P(("groups", "tile"), "row"),
        P("groups", None, None),
        P(("groups", "tile"), "row"),
        P(("groups", "tile"), "row"),
        P("lev", ("groups", "tile"), "row"),
        P(None, "lev"),
        P(),
    )
    tiles, rows, levs = mesh.shape["tile"], mesh.shape["row"], mesh.shape["lev"]
    small = tiles * rows * levs <= SMALL and levs == 2
    return jax.shard_map(
        functools.partial(fused, tiles, rows, levs) if small else shards,
        mesh=mesh,
        in_specs=placed,
        out_specs=(P("lev", ("groups", "tile"), "row"), P(("groups", "tile", "row"), None)),
        check_vma=False,
    )
```

```python
import functools
import jax
import jax.numpy as jnp
from jax import lax
from jax.experimental import pallas as pl
from jax.experimental.pallas import tpu as pltpu
from jax.sharding import PartitionSpec as P

precise = lax.Precision.HIGHEST
f32 = jnp.float32
bf16 = jnp.bfloat16
MESH = pl.DeviceIdType.MESH
FIRST, SECOND, THIRD = (1, 2, 0), (7, 8, 9), (3, 4, 5, 6, 10, 11)
SMALL = 16


def halves(v):
    hi = v.astype(bf16)
    return hi, (v - hi.astype(f32)).astype(bf16)


def iota(shape, dim):
    return lax.broadcasted_iota(jnp.int32, shape, dim)


def dot(a, b):
    return jnp.dot(a, b, preferred_element_type=f32)


def window(
    tiles, rows, levs,
    *refs,
):
    sources, (out_ref, skin_ref), held = refs[:12], refs[12:14], refs[14:26]
    loads = [
        pltpu.make_async_copy(source, target, refs[-1].at[n])
        for n, (source, target) in enumerate(zip(sources, held))
    ]
    for n in FIRST + SECOND + THIRD:
        loads[n].start()
    exchange(tiles, rows, levs, loads, *held, out_ref, skin_ref, *refs[26:-1])


def exchange(
    tiles, rows, levs, loads,
    air_ref, stripes_ref, tally_ref, src_ref, wid_ref, cnt_ref, area_ref, sea_ref, mix_ref,
    warm_ref, factor_ref, thick_ref,
    out_ref, skin_ref,
    outbox, inbox, edge, zin, colbuf, xin, dbuf, sel, sel_t, area_t, area_cat, table, base,
    spread, reply, replies,
    flux_send, flux_recv, halo_send, halo_recv, back_send, back_recv,
):
    tile, row, lev = lax.axis_index("tile"), lax.axis_index("row"), lax.axis_index("lev")
    peers = tiles * rows
    count = peers * levs
    me = (tile * rows + row) * levs + lev
    fields, owned, width = air_ref.shape
    slots = stripes_ref.shape[0]
    depth, lines = warm_ref.shape[:2]
    tables = area_ref.shape[0]
    picks = fields * slots
    places = peers * slots

    def device(o):
        return {"tile": o // (rows * levs), "row": (o // levs) % rows, "lev": o % levs}

    barrier = pltpu.get_barrier_semaphore()
    for j in range(1, count):
        pl.semaphore_signal(barrier, inc=1, device_id=device((me + j) % count), device_id_type=MESH)

    for n in FIRST:
        loads[n].wait()

    live = iota((slots, peers), 0) < tally_ref[...]
    listed = jnp.where(live, stripes_ref[...], -1)
    lane = iota((slots, peers * picks), 1)
    wide = jnp.zeros(lane.shape, jnp.int32)
    for d in range(peers):
        wide = jnp.where(lane // picks == d, listed[:, d : d + 1], wide)
    picked = jnp.sum(
        jnp.where(lane % slots == iota(lane.shape, 0), wide, 0), axis=0, keepdims=True
    )
    total = peers * picks
    at = iota((fields * owned, total), 0)
    to = iota((fields * owned, total), 1)
    chooser = jnp.where(
        jnp.logical_and(at // owned == (to // slots) % fields, at % owned == picked), 1.0, 0.0
    )
    chooser = chooser.T.astype(bf16)
    air_hi, air_lo = halves(air_ref[...].reshape(fields * owned, width))
    outbox[...] = (dot(chooser, air_hi) + dot(chooser, air_lo)).reshape(outbox.shape)

    for n in SECOND:
        loads[n].wait()
    sea = sea_ref[...].astype(f32)
    mix = mix_ref[...]
    edge[...] = jnp.zeros_like(edge)
    for side, line in ((0, 0), (1, lines - 1)):
        for l in range(depth):
            edge[side, l : l + 1, :] = warm_ref[l, line : line + 1, :]
        edge[side, depth : depth + 1, :] = sea[line : line + 1]
        edge[side, depth + 1 : depth + 2, :] = mix[line : line + 1]
    lane = iota((lines, width), 1)
    packed = jnp.zeros((lines, width), f32)
    for l in range(depth):
        packed = jnp.where(lane == l, warm_ref[l, :, 0:1], packed)
        packed = jnp.where(lane == depth + l, warm_ref[l, :, width - 1 : width], packed)
    packed = jnp.where(lane == 2 * depth, sea[:, 0:1], packed)
    packed = jnp.where(lane == 2 * depth + 1, sea[:, width - 1 : width], packed)
    packed = jnp.where(lane == 2 * depth + 2, mix[:, 0:1], packed)
    packed = jnp.where(lane == 2 * depth + 3, mix[:, width - 1 : width], packed)
    colbuf[...] = packed.T[: 3 * depth]

    pl.semaphore_wait(barrier, count - 1)

    def flux(j):
        o = (me + j) % count
        return pltpu.make_async_remote_copy(
            src_ref=outbox.at[o // levs],
            dst_ref=inbox.at[me],
            send_sem=flux_send.at[j],
            recv_sem=flux_recv.at[j],
            device_id=device(o),
            device_id_type=MESH,
        )

    for j in range(1, count):
        flux(j).start()
    inbox[pl.ds(me, 1)] = outbox[pl.ds(me // levs, 1)]

    halos = (
        (0, tile > 0, tile < tiles - 1, edge.at[0], zin.at[1], {"tile": jnp.maximum(tile - 1, 0)}),
        (1, tile < tiles - 1, tile > 0, edge.at[1], zin.at[0], {"tile": jnp.minimum(tile + 1, tiles - 1)}),
        (2, row > 0, row < rows - 1, colbuf, xin.at[1], {"row": jnp.maximum(row - 1, 0)}),
        (3, row < rows - 1, row > 0, colbuf, xin.at[0], {"row": jnp.minimum(row + 1, rows - 1)}),
    )

    def halo(i):
        n, there, comes, src, dst, target = halos[i]
        return pltpu.make_async_remote_copy(
            src_ref=src,
            dst_ref=dst,
            send_sem=halo_send.at[n],
            recv_sem=halo_recv.at[n],
            device_id=target,
            device_id_type=MESH,
        )

    for i in range(4):
        pl.when(halos[i][1])(lambda i=i: halo(i).start())

        @pl.when(jnp.logical_not(halos[i][2]))
        def _(i=i):
            halos[i][4][...] = jnp.zeros(halos[i][4].shape, f32)

    for n in THIRD:
        loads[n].wait()

    entry = iota((tables * places, lines), 0)
    counts = jnp.zeros((tables * places, lines), f32)
    for k in range(src_ref.shape[0]):
        ident = jnp.where(
            k < cnt_ref[...], wid_ref[k : k + 1, :] * places + src_ref[k : k + 1, :], -1
        )
        counts = counts + jnp.where(entry == ident, 1.0, 0.0)
    sel_t[...] = counts.astype(bf16)
    counts = counts.T.astype(bf16)
    sel[:, : tables * places] = counts
    sel[:, tables * places :] = counts

    for w in range(tables):
        hi, lo = halves(area_ref[w])
        area_cat[w * width : (w + 1) * width, :width] = hi
        area_cat[w * width : (w + 1) * width, width:] = lo
        hi, lo = halves(area_ref[w].T)
        area_t[0:width, w * width : (w + 1) * width] = hi
        area_t[width : 2 * width, w * width : (w + 1) * width] = lo

    ones = jnp.ones((places, 2 * width), bf16)
    sums = dot(ones, area_t[: 2 * width, :])
    for w in range(tables):
        hi, lo = halves(sums[:, w * width : (w + 1) * width])
        table[w * places : (w + 1) * places, :width] = hi
        table[(tables + w) * places : (tables + w + 1) * places, :width] = lo
    heat_scale = sea / dot(sel[...], table[:, :width])

    def backward(values):
        for w in range(tables):
            hi, lo = halves(values[w * places : (w + 1) * places])
            spread[:places, w * width : (w + 1) * width] = hi
            spread[places:, w * width : (w + 1) * width] = lo
        r = dot(spread[...], area_cat[...])
        return (r[:places, :width] + r[:places, width:]) + (r[places:, :width] + r[places:, width:])

    den = backward(dot(sel_t[...], sea.astype(bf16))) * (1.0 / levs)
    for p in range(peers):
        reply[p, slots : 2 * slots, :] = den[p * slots : (p + 1) * slots]

    size = peers * levs * picks
    by_level = jnp.where(iota((depth * places, depth), 0) // places == iota((depth * places, depth), 1), 1.0, 0.0)
    by_field = jnp.where(
        (iota((levs * fields, size), 1) // slots) % (levs * fields) == iota((levs * fields, size), 0), 1.0, 0.0
    )
    mixer = lax.dot_general(
        by_level, factor_ref[...], (((1,), (1,)), ((), ())), precision=precise, preferred_element_type=f32
    )
    mixer = jnp.dot(mixer, by_field, precision=precise, preferred_element_type=f32)
    r = iota((depth * places, size), 0)
    c = iota((depth * places, size), 1)
    same = jnp.logical_and((r // slots) % peers == c // (levs * picks), r % slots == c % slots)
    mix_hi, mix_lo = halves(jnp.where(same, mixer, 0.0))

    right = 0.5 * (mix + pltpu.roll(mix, width - 1, 1)) * sea * pltpu.roll(sea, width - 1, 1)
    right = jnp.where(lane == width - 1, 0.0, right)
    line = iota((lines, width), 0)
    down = 0.5 * (mix + pltpu.roll(mix, lines - 1, 0)) * sea * pltpu.roll(sea, lines - 1, 0)
    down = jnp.where(line == lines - 1, 0.0, down)
    for i in range(4):
        pl.when(halos[i][2])(lambda i=i: halo(i).wait_recv())
    side = []
    for n, edge_line in ((0, 0), (1, lines - 1)):
        coef = (
            edge[n, depth : depth + 1, :] * zin[n, depth : depth + 1, :] * 0.5
            * (edge[n, depth + 1 : depth + 2, :] + zin[n, depth + 1 : depth + 2, :])
        )
        side.append(coef * (zin[n, :depth, :] - edge[n, :depth, :]))
    dbuf[...] = jnp.zeros_like(dbuf)
    for n in range(2):
        o = 1 - n
        coef = (
            colbuf[2 * depth + n : 2 * depth + n + 1, :]
            * xin[n, 2 * depth + o : 2 * depth + o + 1, :]
            * 0.5
            * (
                colbuf[2 * depth + 2 + n : 2 * depth + 3 + n, :]
                + xin[n, 2 * depth + 2 + o : 2 * depth + 3 + o, :]
            )
        )
        dbuf[n * depth : (n + 1) * depth, :] = coef * (
            xin[n, o * depth : (o + 1) * depth, :] - colbuf[n * depth : (n + 1) * depth, :]
        )
    columns = dbuf[...].T
    for l in range(depth):
        heat = warm_ref[l]
        east = right * (pltpu.roll(heat, width - 1, 1) - heat)
        south = down * (pltpu.roll(heat, lines - 1, 0) - heat)
        moved = heat + ((east - pltpu.roll(east, 1, 1)) + (south - pltpu.roll(south, 1, 0)))
        moved = moved + jnp.where(lane == 0, columns[:, l : l + 1], 0.0)
        moved = moved + jnp.where(lane == width - 1, columns[:, depth + l : depth + l + 1], 0.0)
        moved = moved + jnp.where(line == 0, side[0][l : l + 1], 0.0)
        base[l] = moved + jnp.where(line == lines - 1, side[1][l : l + 1], 0.0)

    for j in range(1, count):
        flux(j).wait_recv()
    got_hi, got_lo = halves(inbox[...].reshape(size, width))
    level_flux = dot(mix_hi, got_hi) + (dot(mix_hi, got_lo) + dot(mix_lo, got_hi))
    g_hi, g_lo = halves(level_flux)
    for w in range(0, tables, 2):
        at = slice(w * width, (w + 2) * width)
        part = dot(g_hi, area_t[:width, at]) + (
            dot(g_hi, area_t[width : 2 * width, at]) + dot(g_lo, area_t[:width, at])
        )
        hi, lo = halves(part)
        for n in range(2):
            for l in range(depth):
                put = slice((w + n) * places, (w + n + 1) * places)
                put_lo = slice((tables + w + n) * places, (tables + w + n + 1) * places)
                rows_l = slice(l * places, (l + 1) * places)
                cols_l = slice(n * width, (n + 1) * width)
                table[put, l * width : (l + 1) * width] = hi[rows_l, cols_l]
                table[put_lo, l * width : (l + 1) * width] = lo[rows_l, cols_l]
    thick_sum = thick_ref[0]
    for l in range(1, levs * depth):
        thick_sum = thick_sum + thick_ref[l]
    surface = jnp.zeros((lines, width), f32)
    for l in range(0, depth, 2):
        heating = dot(sel[...], table[:, l * width : (l + 2) * width])
        for n in range(2):
            heat = base[l + n] + heat_scale * heating[:, n * width : (n + 1) * width]
            out_ref[l + n] = heat
            surface = surface + thick_ref[lev * depth + l + n] * heat
    surface = sea * surface / thick_sum

    hi, lo = halves(surface)
    num = backward(dot(sel_t[...], hi) + dot(sel_t[...], lo))
    for p in range(peers):
        reply[p, :slots, :] = num[p * slots : (p + 1) * slots]

    def back(j):
        o = (me + j) % count
        return pltpu.make_async_remote_copy(
            src_ref=reply.at[o // levs],
            dst_ref=replies.at[me],
            send_sem=back_send.at[j],
            recv_sem=back_recv.at[j],
            device_id=device(o),
            device_id_type=MESH,
        )

    for j in range(1, count):
        back(j).start()
    replies[pl.ds(me, 1)] = reply[pl.ds(me // levs, 1)]
    at = iota((2 * owned, total), 0)
    to = iota((2 * owned, total), 1)
    gather = jnp.where(
        jnp.logical_and(at % owned == picked, at // owned == (to % (2 * slots)) // slots), 1.0, 0.0
    ).astype(bf16)
    for j in range(1, count):
        back(j).wait_recv()
    hi, lo = halves(replies[...].reshape(total, width))
    sums = dot(gather, hi) + dot(gather, lo)
    skin_ref[...] = sums[:owned] / jnp.maximum(sums[owned:], 1.0)

    for j in range(1, count):
        flux(j).wait_send()
        back(j).wait_send()
    for i in range(4):
        pl.when(halos[i][1])(lambda i=i: halo(i).wait_send())


def fused(
    tiles, rows, levs,
    air_exchange_rates, outgoing_stripes, outgoing_tally, regrid_inputs, regrid_factor_id,
    regrid_tally, intersection_areas, sea_indicator, mixing_rate, warmth_profile,
    warming_factor, stratum_depths,
):
    fields, owned, width = air_exchange_rates.shape
    slots = outgoing_stripes.shape[2]
    depth, lines = warmth_profile.shape[:2]
    tables = intersection_areas.shape[0]
    peers = tiles * rows
    count = peers * levs
    places = peers * slots
    vmem = pl.BlockSpec(memory_space=pltpu.VMEM)
    operands = (
        air_exchange_rates,
        outgoing_stripes[0].T,
        outgoing_tally,
        regrid_inputs[:, 0, :].T,
        regrid_factor_id[:, 0, :].T,
        regrid_tally.T,
        intersection_areas,
        sea_indicator,
        mixing_rate,
        warmth_profile,
        warming_factor,
        stratum_depths,
    )
    dma = pltpu.SemaphoreType.DMA
    return pl.pallas_call(
        functools.partial(window, tiles, rows, levs),
        out_shape=(
            pltpu.VMEM(warmth_profile.shape, f32),
            pltpu.VMEM((owned, width), f32),
        ),
        in_specs=[pl.BlockSpec(memory_space=pltpu.HBM)] * 12,
        out_specs=(vmem, vmem),
        scratch_shapes=[pltpu.VMEM(x.shape, x.dtype) for x in operands[:11]]
        + [pltpu.SMEM(stratum_depths.shape, f32)]
        + [
            pltpu.VMEM((peers, fields * slots, width), f32),
            pltpu.VMEM((count, fields * slots, width), f32),
            pltpu.VMEM((2, 2 * depth, width), f32),
            pltpu.VMEM((2, 2 * depth, width), f32),
            pltpu.VMEM((3 * depth, lines), f32),
            pltpu.VMEM((2, 3 * depth, lines), f32),
            pltpu.VMEM((width, lines), f32),
            pltpu.VMEM((lines, 2 * tables * places), bf16),
            pltpu.VMEM((tables * places, lines), bf16),
            pltpu.VMEM((2 * width, tables * width), bf16),
            pltpu.VMEM((tables * width, 2 * width), bf16),
            pltpu.VMEM((2 * tables * places, depth * width), bf16),
            pltpu.VMEM((depth, lines, width), f32),
            pltpu.VMEM((2 * places, tables * width), bf16),
            pltpu.VMEM((peers, 2 * slots, width), f32),
            pltpu.VMEM((count, 2 * slots, width), f32),
            dma((count,)), dma((count,)), dma((4,)), dma((4,)), dma((count,)), dma((count,)),
            dma((12,)),
        ],
        compiler_params=pltpu.CompilerParams(
            collective_id=0, has_side_effects=True, vmem_limit_bytes=60 * 1024 * 1024
        ),
        name="window",
    )(*operands)


def extended(cells, sides, width):
    for axis, dim in sides:
        count = lax.axis_size(axis)
        ends = count - 1
        head = lax.slice_in_dim(cells, 0, width, axis=dim)
        tail = lax.slice_in_dim(cells, cells.shape[dim] - width, cells.shape[dim], axis=dim)
        cells = jnp.concatenate(
            [
                lax.ppermute(tail, axis, [(i, (i + 1) % count) for i in range(ends)]),
                cells,
                lax.ppermute(head, axis, [((i + 1) % count, i) for i in range(ends)]),
            ],
            axis=dim,
        )
    return cells


def shards(
    air_exchange_rates,
    outgoing_stripes,
    outgoing_tally,
    regrid_inputs,
    regrid_factor_id,
    regrid_tally,
    intersection_areas,
    sea_indicator,
    mixing_rate,
    warmth_profile,
    warming_factor,
    stratum_depths,
):
    tile_count = lax.axis_size("tile")
    row_count = lax.axis_size("row")
    peer_count = tile_count * row_count
    field_count, atm_rows, width = air_exchange_rates.shape
    slot_count = outgoing_stripes.shape[2]
    marine_stripes = warmth_profile.shape[1]
    depth_tally = warmth_profile.shape[0]
    block_most = regrid_inputs.shape[2]
    table_size = intersection_areas.shape[0]
    row_list = outgoing_stripes[0].reshape(-1)
    live_slot = (
        (jnp.arange(slot_count, dtype=jnp.int32)[None, :] < outgoing_tally[0][:, None])
        .reshape(-1)
        .astype(jnp.float32)
    )
    picker = (row_list[:, None] == jnp.arange(atm_rows, dtype=jnp.int32)[None, :]).astype(
        jnp.float32
    ) * live_slot[:, None]
    outgoing = jnp.einsum("qa,fac->qfc", picker, air_exchange_rates, precision=precise)
    arrived = lax.all_to_all(outgoing, ("tile", "row"), split_axis=0, concat_axis=0, tiled=True)
    source_slot = regrid_inputs[:, 0, :]
    weight_id = regrid_factor_id[:, 0, :]
    block_count = regrid_tally[:, 0]
    usable = (jnp.arange(block_most, dtype=jnp.int32)[None, :] < block_count[:, None]).astype(
        jnp.float32
    )
    selector = (
        weight_id[:, :, None] == jnp.arange(table_size, dtype=jnp.int32)[None, None, :]
    ).astype(jnp.float32) * usable[:, :, None]
    fetched = arrived[source_slot]
    grouped = jnp.einsum("xkw,xkfc->wxfc", selector, fetched, precision=precise)
    summed = jnp.einsum("wec,wxfc->fxe", intersection_areas, grouped, precision=precise)
    coverage = jnp.einsum(
        "xkw,we->xe", selector, jnp.sum(intersection_areas, axis=2), precision=precise
    )
    local_flux = summed / coverage[None]
    all_flux = lax.all_gather(local_flux, "lev", axis=0, tiled=True)
    thermal_tendency = jnp.einsum("fl,fxc->lxc", warming_factor, all_flux, precision=precise)
    marine_indicator = sea_indicator.astype(jnp.float32)
    piled_arrays = jnp.concatenate(
        [warmth_profile, marine_indicator[None], mixing_rate[None]], axis=0
    )
    padded = extended(piled_arrays, (("tile", 1), ("row", 2)), 1)
    spread_tracer = jnp.zeros_like(warmth_profile)
    for step_x, step_y in ((1, 0), (-1, 0), (0, 1), (0, -1)):
        neighbour_values = padded[
            :, 1 + step_x : 1 + step_x + marine_stripes, 1 + step_y : 1 + step_y + width
        ]
        spread_tracer = spread_tracer + neighbour_values[depth_tally] * 0.5 * (
            mixing_rate + neighbour_values[depth_tally + 1]
        ) * (neighbour_values[:depth_tally] - warmth_profile)
    warmth_following = warmth_profile + marine_indicator * (spread_tracer + thermal_tendency)
    level_start = lax.axis_index("lev") * depth_tally
    own_thick = lax.dynamic_slice_in_dim(stratum_depths, level_start, depth_tally)
    partial_value = jnp.einsum(
        "l,lxc->xc", own_thick, warmth_following, precision=precise
    ) / jnp.sum(stratum_depths)
    topmost_stratum = lax.psum(partial_value, "lev")
    columns = intersection_areas.shape[2]
    coupled_entries = jnp.stack([marine_indicator * topmost_stratum, marine_indicator], axis=1)
    spread = jnp.einsum("wec,xje->wxjc", intersection_areas, coupled_entries, precision=precise)
    contribution = jnp.einsum("xkw,wxjc->xkjc", selector, spread, precision=precise)
    target = (
        source_slot.reshape(-1)[:, None]
        == jnp.arange(peer_count * slot_count, dtype=jnp.int32)[None, :]
    ).astype(jnp.float32)
    returning = jnp.einsum(
        "rq,rjc->qjc",
        target,
        contribution.reshape(marine_stripes * block_most, 2, columns),
        precision=precise,
    )
    returned = lax.all_to_all(
        returning.reshape(peer_count, slot_count, 2, columns),
        ("tile", "row"),
        split_axis=0,
        concat_axis=0,
        tiled=True,
    )
    returned = returned.reshape(peer_count * slot_count, 2, columns)
    atm_sums = jnp.einsum("qa,qjc->ajc", picker, returned, precision=precise)
    dividend_sum = atm_sums[:, 0]
    divisor_sum = atm_sums[:, 1]
    air_side_skin_heat = dividend_sum / jnp.maximum(divisor_sum, 1.0)
    return (warmth_following, air_side_skin_heat)


def solution(mesh):
    placed = (
        P("lev", ("groups", "tile", "row"), None),
        P(("groups", "tile", "row"), None, None),
        P(("groups", "tile", "row"), None),
        P(("groups", "tile"), "row", None),
        P(("groups", "tile"), "row", None),
        P(("groups", "tile"), "row"),
        P("groups", None, None),
        P(("groups", "tile"), "row"),
        P(("groups", "tile"), "row"),
        P("lev", ("groups", "tile"), "row"),
        P(None, "lev"),
        P(),
    )
    tiles, rows, levs = mesh.shape["tile"], mesh.shape["row"], mesh.shape["lev"]
    small = tiles * rows * levs <= SMALL and levs == 2
    return jax.shard_map(
        functools.partial(fused, tiles, rows, levs) if small else shards,
        mesh=mesh,
        in_specs=placed,
        out_specs=(P("lev", ("groups", "tile"), "row"), P(("groups", "tile", "row"), None)),
        check_vma=False,
    )
```
